128 devices in a mesh: rep: 64 (over z, y_hi, x, core), fsdp: 2 (over y_lo).
Axes of the slice: x: 4, y: 4 (y_hi: 2, y_lo: 2; y = y_hi * 2 + y_lo), z: 4, core: 2. Of those that a mesh axis runs over, the one named last changes fastest.
Arguments:
- activations: bfloat16 [32768, 576], P(('rep', 'fsdp')), may hold values from -6 to 6
- seg_ids: int32 [128, 256], P(('rep', 'fsdp')), may hold values from 0 to 3, never falling along the last dimension, each value on 1 to 128 neighbouring positions
- cotangent: bfloat16 [32768, 576], P(('rep', 'fsdp')), may hold values from -6 to 6
- attend_gain: bfloat16 [2, 576], P(None, 'fsdp'), may hold values from 0.5 to 1.5
- query_weight: bfloat16 [2, 576, 576], P(None, 'fsdp'), may hold values from -0.25 to 0.25
- key_matrix: bfloat16 [2, 576, 192], P(None, 'fsdp'), may hold values from -0.25 to 0.25
- value_matrix: bfloat16 [2, 576, 192], P(None, 'fsdp'), may hold values from -0.25 to 0.25
- output_weight: bfloat16 [2, 576, 576], P(None, 'fsdp'), may hold values from -0.75 to 0.75
- mixer_gain: bfloat16 [2, 576], P(None, 'fsdp'), may hold values from 0.5 to 1.5
- gate_weight: bfloat16 [2, 576, 1536], P(None, 'fsdp'), may hold values from -0.25 to 0.25
- up_weight: bfloat16 [2, 576, 1536], P(None, 'fsdp'), may hold values from -0.25 to 0.25
- down_weight: bfloat16 [2, 1536, 576], P(None, 'fsdp'), may hold values from -0.15625 to 0.15625
Outputs:
- layer_output: bfloat16 [32768, 576], P(('rep', 'fsdp'))
- input_grad: float32 [32768, 576], P(('rep', 'fsdp'))
- attend_grad: float32 [2, 576], P(None, 'fsdp')
- query_grad: float32 [2, 576, 576], P(None, 'fsdp')
- key_grad: float32 [2, 576, 192], P(None, 'fsdp')
- value_grad: float32 [2, 576, 192], P(None, 'fsdp')
- output_grad: float32 [2, 576, 576], P(None, 'fsdp')
- mixer_grad: float32 [2, 576], P(None, 'fsdp')
- gate_grad: float32 [2, 576, 1536], P(None, 'fsdp')
- up_grad: float32 [2, 576, 1536], P(None, 'fsdp')
- down_grad: float32 [2, 1536, 576], P(None, 'fsdp')
The draws below stay inside these ranges and needn't reach their ends.
Inputs may be any that keep to these rules, and one draw needn't show every extreme that they name: `seg_ids`: within each row of 256 tokens the numbers never fall; a run of equal numbers is one document of 1 to 128 tokens.
All inputs are finite; a program needn't handle non-finite values.
Results may differ from the reference program's by a relative error of at most 0.023.
Values may be sent and summed in bfloat16 or wider, within the bound.
No kernel may reach another device: no remote copies, remote signals or barrier semaphores. Data moves between devices by JAX's collectives and lax.ppermute only.
A program may use at most 192 MiB of HBM per device.

```python
import math
import jax
import jax.numpy as jnp
import numpy as np
from jax import lax

MODEL_WIDTH = 576
FF = 1536
QUERY_HEADS = 9
KEY_VALUE_HEADS = 3
HEAD_WIDTH = 64
DECODER_LAYERS = 2
SEGS = 4
TOK_DEV = 256
TOKENS = 32768
DEVICES = 128


def level_of(stream_key, extent, cuts, least, high):
    gain, own = 1.0, jax.random.fold_in(stream_key, 6)
    for dim, shards_of in cuts:
        steps = jnp.exp(jax.random.uniform(jax.random.fold_in(own, dim), (shards_of,), jnp.float32, least / len(cuts), high / len(cuts)))
        gain = gain * jnp.repeat(steps, extent[dim] // shards_of).reshape([-1 if axis == dim else 1 for axis in range(len(extent))])
    return gain


def split_up(number_of, total, most, slope):
    weights = [(1 << 20) // math.isqrt(rank ** slope) + 1 for rank in range(2, number_of + 1)]
    surplus, counts = total - most - (number_of - 1), [1] * (number_of - 1)
    while surplus > 0:
        candidates = [i for i in range(number_of - 1) if counts[i] < most]
        whole, budget = sum([weights[i] for i in candidates]), surplus
        for i in candidates:
            addition = min(most - counts[i], max(1, budget * weights[i] // whole), surplus)
            counts[i] = counts[i] + addition
            surplus = surplus - addition
    return np.array([most] + counts)


def uneven_parts(own_key, number_of, total, bound, skew):
    if number_of == 2:
        one = jax.random.randint(own_key, (), max(1, total - bound), min(bound, total - 1) + 1)
        return jnp.stack([one, total - one])
    lengths = jnp.asarray(split_up(number_of, total, bound, skew), jnp.int32)
    pairs = (number_of - 1) // 2
    source_of, taker = lengths[1:1 + 2 * pairs:2], lengths[2:2 + 2 * pairs:2]
    margin = jnp.minimum(source_of - 1, bound - taker)
    shifted = jax.random.randint(jax.random.fold_in(own_key, 1), (pairs,), 0, 1 << 20) % (margin + 1)
    lengths = lengths.at[1:1 + 2 * pairs:2].set(source_of - shifted).at[2:2 + 2 * pairs:2].set(taker + shifted)
    return lengths[jax.random.permutation(jax.random.fold_in(own_key, 2), number_of)]


def bell_draw(own_key, dims, spread, most, split=(), kind=jnp.bfloat16):
    factor_of = level_of(own_key, dims, split, -0.22, 0.18) if split else 1.0
    array = jax.random.normal(own_key, dims, jnp.float32) * spread * factor_of
    return jnp.minimum(jnp.maximum(array, -most), most).astype(kind)


def setup_inputs(seed: int = 0) -> dict:
    streams_of = jax.random.split(jax.random.key(seed), 13)
    activations = bell_draw(streams_of[0], (TOKENS, MODEL_WIDTH), 1.0, 6.0, ((0, 128),))
    seg_ids = jax.vmap(lambda own: jnp.searchsorted(jnp.cumsum(uneven_parts(own, SEGS, TOK_DEV, TOK_DEV // 2, 1)), jnp.arange(TOK_DEV), side="right"))(jax.random.split(streams_of[1], DEVICES)).reshape((DEVICES, TOK_DEV)).astype(jnp.int32)
    cotangent = bell_draw(streams_of[2], (TOKENS, MODEL_WIDTH), 1.0, 6.0, ((0, 128),))
    attend_gain = jnp.clip(1.0 + 0.1 * jax.random.normal(streams_of[3], (DECODER_LAYERS, MODEL_WIDTH), jnp.float32), 0.5, 1.5).astype(jnp.bfloat16)
    query_weight = bell_draw(streams_of[4], (DECODER_LAYERS, MODEL_WIDTH, MODEL_WIDTH), MODEL_WIDTH ** -0.5, 0.25, ((1, 2),))
    key_matrix = bell_draw(streams_of[5], (DECODER_LAYERS, MODEL_WIDTH, KEY_VALUE_HEADS * HEAD_WIDTH), MODEL_WIDTH ** -0.5, 0.25, ((1, 2),))
    value_matrix = bell_draw(streams_of[6], (DECODER_LAYERS, MODEL_WIDTH, KEY_VALUE_HEADS * HEAD_WIDTH), MODEL_WIDTH ** -0.5, 0.25, ((1, 2),))
    output_weight = bell_draw(streams_of[7], (DECODER_LAYERS, MODEL_WIDTH, MODEL_WIDTH), (MODEL_WIDTH // 8) ** -0.5, 0.75, ((1, 2),))
    mixer_gain = jnp.clip(1.0 + 0.1 * jax.random.normal(streams_of[8], (DECODER_LAYERS, MODEL_WIDTH), jnp.float32), 0.5, 1.5).astype(jnp.bfloat16)
    gate_weight = bell_draw(streams_of[9], (DECODER_LAYERS, MODEL_WIDTH, FF), MODEL_WIDTH ** -0.5, 0.25, ((1, 2),))
    up_weight = bell_draw(streams_of[10], (DECODER_LAYERS, MODEL_WIDTH, FF), MODEL_WIDTH ** -0.5, 0.25, ((1, 2),))
    down_weight = bell_draw(streams_of[11], (DECODER_LAYERS, FF, MODEL_WIDTH), FF ** -0.5, 0.15625, ((1, 2),))
    return {"activations": activations, "seg_ids": seg_ids, "cotangent": cotangent, "attend_gain": attend_gain, "query_weight": query_weight, "key_matrix": key_matrix, "value_matrix": value_matrix, "output_weight": output_weight, "mixer_gain": mixer_gain, "gate_weight": gate_weight, "up_weight": up_weight, "down_weight": down_weight}


@jax.custom_vjp
def lowered_value(v):
    return lax.optimization_barrier(v.astype(jnp.bfloat16)).astype(jnp.float32)

@jax.custom_vjp
def lowered_backward(v):
    return v

def low_keep(v):
    return (lowered_value(v), None)

def low_pass(kept, grad):
    return (grad,)

def back_keep(v):
    return (v, None)

def back_low(kept, grad):
    return (lowered_value(grad),)
lowered_value.defvjp(low_keep, low_pass)
lowered_backward.defvjp(back_keep, back_low)
highest_precision = lax.Precision.HIGHEST
norm_epsilon = 1e-05
rope_base = 100000.0

def normalize(stream, gain_row):
    return stream * lax.rsqrt(lax.optimization_barrier(jnp.mean(stream * stream, axis=-1, keepdims=True)) + norm_epsilon) * gain_row

def rotate_halves(vectors, cosine_lookup, sine_lookup):
    half_size = vectors.shape[-1] // 2
    first_half = vectors[..., :half_size]
    second_half = vectors[..., half_size:]
    return jnp.concatenate([first_half * cosine_lookup - second_half * sine_lookup, second_half * cosine_lookup + first_half * sine_lookup], axis=-1)

def attend_tokens(block_args):
    query_vectors, keys_block, values_block, document_list = block_args
    count_of_rows = query_vectors.shape[0]
    grouped_heads = query_vectors.reshape(count_of_rows, KEY_VALUE_HEADS, QUERY_HEADS // KEY_VALUE_HEADS, HEAD_WIDTH)
    scores = lowered_backward(jnp.einsum('qkgd,skd->kgqs', grouped_heads, keys_block, precision=highest_precision) * HEAD_WIDTH ** (-0.5))
    row_index = jnp.arange(count_of_rows, dtype=jnp.int32)
    allowed = (document_list[:, None] == document_list[None, :]) & (row_index[None, :] <= row_index[:, None])
    scores = jnp.where(allowed[None, None], scores, -1e+30)
    row_peak = lax.optimization_barrier(jnp.max(scores, axis=-1, keepdims=True))
    exponent = jnp.exp(scores - row_peak)
    probabilities = lowered_value(exponent / lax.optimization_barrier(jnp.sum(exponent, axis=-1, keepdims=True)))
    mixed_heads = jnp.einsum('kgqs,skd->qkgd', probabilities, values_block, precision=highest_precision)
    return mixed_heads.reshape(count_of_rows, QUERY_HEADS * HEAD_WIDTH)

def decoder_layer(stream, layer_weights, cosine_lookup, sine_lookup, document_list, rows_per_block):
    attend_gain, query_weight, key_matrix, value_matrix, output_weight, mixer_gain, gate_weight, up_weight, down_weight = layer_weights
    count_of_rows = stream.shape[0]
    block_list = count_of_rows // rows_per_block
    first_normed = lowered_value(normalize(stream, attend_gain))
    query_vectors = lowered_value(rotate_halves(lowered_backward(jnp.dot(first_normed, query_weight, precision=highest_precision)).reshape(count_of_rows, QUERY_HEADS, HEAD_WIDTH), cosine_lookup, sine_lookup))
    every_key = lowered_value(rotate_halves(lowered_backward(jnp.dot(first_normed, key_matrix, precision=highest_precision)).reshape(count_of_rows, KEY_VALUE_HEADS, HEAD_WIDTH), cosine_lookup, sine_lookup))
    every_value = lowered_value(lowered_backward(jnp.dot(first_normed, value_matrix, precision=highest_precision))).reshape(count_of_rows, KEY_VALUE_HEADS, HEAD_WIDTH)
    attended_rows = lax.map(jax.checkpoint(attend_tokens), (query_vectors.reshape(block_list, rows_per_block, QUERY_HEADS, HEAD_WIDTH), every_key.reshape(block_list, rows_per_block, KEY_VALUE_HEADS, HEAD_WIDTH), every_value.reshape(block_list, rows_per_block, KEY_VALUE_HEADS, HEAD_WIDTH), document_list.reshape(block_list, rows_per_block)))
    attended_rows = lowered_value(lowered_backward(attended_rows.reshape(count_of_rows, QUERY_HEADS * HEAD_WIDTH)))
    middle = stream + lowered_backward(jnp.dot(attended_rows, output_weight, precision=highest_precision))
    normed_two = lowered_value(normalize(middle, mixer_gain))
    gate = lowered_backward(jnp.dot(normed_two, gate_weight, precision=highest_precision))
    upward = lowered_backward(jnp.dot(normed_two, up_weight, precision=highest_precision))
    mixed = lowered_value(jax.nn.silu(gate) * upward)
    return middle + lowered_backward(jnp.dot(mixed, down_weight, precision=highest_precision))

def reference(activations, seg_ids, cotangent, attend_gain, query_weight, key_matrix, value_matrix, output_weight, mixer_gain, gate_weight, up_weight, down_weight):
    row_total = activations.shape[0]
    device_rows = seg_ids.shape[0]
    token_index = jnp.arange(TOK_DEV, dtype=jnp.int32)
    fresh = jnp.concatenate([jnp.ones((device_rows, 1), dtype=bool), seg_ids[:, 1:] != seg_ids[:, :-1]], axis=1)
    starts = lax.cummax(jnp.where(fresh, token_index[None, :], 0), axis=1)
    positions = (token_index[None, :] - starts).reshape(row_total).astype(jnp.float32)
    frequency = rope_base ** (-(jnp.arange(HEAD_WIDTH // 2, dtype=jnp.float32) * 2.0 / HEAD_WIDTH))
    angles = positions[:, None] * frequency[None, :]
    cosine_lookup = jnp.cos(angles)[:, None, :]
    sine_lookup = jnp.sin(angles)[:, None, :]
    document_list = (seg_ids + jnp.arange(device_rows, dtype=jnp.int32)[:, None] * SEGS).reshape(row_total)
    rows_per_block = TOK_DEV * max(1, 512 // TOK_DEV)
    weight_list = (attend_gain, query_weight, key_matrix, value_matrix, output_weight, mixer_gain, gate_weight, up_weight, down_weight)
    floats = tuple((weight_array.astype(jnp.float32) for weight_array in weight_list))

    def forward(stream, *stacked):
        for layer_index in range(DECODER_LAYERS):
            stream = decoder_layer(stream, tuple((weight_array[layer_index] for weight_array in stacked)), cosine_lookup, sine_lookup, document_list, rows_per_block)
        return stream
    result, pullback = jax.vjp(forward, activations.astype(jnp.float32), *floats)
    grads = pullback(cotangent.astype(jnp.float32))
    return (result.astype(jnp.bfloat16), grads[0], grads[1], grads[2], grads[3], grads[4], grads[5], grads[6], grads[7], grads[8], grads[9])
```

```python
import functools

import jax
import jax.numpy as jnp
from jax import lax
from jax.experimental import pallas as pl
from jax.experimental.pallas import tpu as pltpu
from jax.sharding import PartitionSpec as P

F32 = jnp.float32
BF16 = jnp.bfloat16
ROWS = 256
WIDTH = 576
FF = 1536
HEAD = 64
EPSILON = 1e-05
ROPE_BASE = 100000.0
MASKED = -1e30
SCALE = HEAD**-0.5
STEP = 256

ALL = ("z", "yh", "x", "core", "yl")
SIZES = (4, 2, 4, 2, 2)
WEIGHT_SHAPES = ((576, 576), (576, 192), (576, 192), (576, 576), (576, 1536), (576, 1536), (576, 1536))
TILES = (38, 36, 36)
BLOCKS = [(i, 0, c, min(128, WEIGHT_SHAPES[i][1] - c)) for i in range(6) for c in range(0, WEIGHT_SHAPES[i][1], 128)]
BLOCKS += [(6, r, c, 128) for r in range(0, 576, 144) for c in range(0, 384, 128)]
QUARTERS = (BLOCKS[:25], BLOCKS[25:])
CHUNKS = (((0, 25),), ((0, 25),))
VMEM_LIMIT = 50 * 2**20
LAST_VMEM = 30 * 2**20
LATE = pltpu.CompilerParams(vmem_limit_bytes=LAST_VMEM)

PACK_VMEM = 60 * 2**20
ORDERS = (("y", "x", "z"), ("z", "y", "x"), ("x", "z", "y"))
STEPS = (("y", "xu", "zu"), ("zu", "y", "xu"), ("xu", "zu", "y"))


def coordinates(index):
    out = []
    for size in reversed(SIZES):
        out.append(index % size)
        index //= size
    return tuple(reversed(out))


def place(z, yh, x, core, yl):
    return (((z * 2 + yh) * 4 + x) * 2 + core) * 2 + yl


def move_y(z, yh, x, core, yl):
    y = yh * 2 + yl
    y = y ^ 1 if core == 0 else 3 - y
    return (z, y // 2, x, core, y % 2)


def move_yh(z, yh, x, core, yl):
    return (z, 1 - yh, x, core, yl)


def move_core(z, yh, x, core, yl):
    return (z, yh, x, 1 - core, yl)


def ring_step(at, low):
    return at ^ 1 if low else 3 - at


def move_x(first, z, yh, x, core, yl):
    return (z, yh, ring_step(x, first == (core == 0)), core, yl)


def move_z(first, z, yh, x, core, yl):
    return (ring_step(z, first == (core == 0)), yh, x, core, yl)


MOVES = {
    "y": move_y,
    "yh": move_yh,
    "core": move_core,
    "xu": functools.partial(move_x, True),
    "xv": functools.partial(move_x, False),
    "zu": functools.partial(move_z, True),
    "zv": functools.partial(move_z, False),
    "xzv": lambda *at: move_x(False, *move_z(False, *at)),
}


def swap(a, move):
    return lax.ppermute(a, ALL, [(i, place(*MOVES[move](*coordinates(i)))) for i in range(128)])


def dot(a, b):
    return lax.dot_general(a, b, (((1,), (0,)), ((), ())), preferred_element_type=F32)


def dot_nt(a, b):
    return lax.dot_general(a, b, (((1,), (1,)), ((), ())), preferred_element_type=F32)


def dot_tn(a, b):
    return lax.dot_general(a, b, (((0,), (0,)), ((), ())), preferred_element_type=F32)


def factor_of(x):
    return lax.rsqrt(jnp.mean(x * x, axis=-1, keepdims=True) + EPSILON)


def sigmoid(u):
    return 0.5 * jnp.tanh(0.5 * u) + 0.5


def swapped_halves(chunk):
    lane = lax.broadcasted_iota(jnp.int32, chunk.shape, 1)
    return jnp.where(lane % HEAD < HEAD // 2, pltpu.roll(chunk, 96, 1), pltpu.roll(chunk, 32, 1))


def heads_of(ref, group):
    return jnp.concatenate([ref[:, HEAD * h : HEAD * (h + 1)] for h in range(3 * group, 3 * group + 3)], axis=0)


def weight_copies(layer, scal, own, held, sems, which=range(7)):
    yl = scal[0]
    copies = [[] for _ in range(7)]
    for i in which:
        if i < 6:
            to = held[i].at[pl.ds(pl.multiple_of(yl * 288, 16), 288), :]
        else:
            to = held[i].at[:, pl.ds(pl.multiple_of(yl * 768, 128), 768)]
        copies[i] = [pltpu.make_async_copy(own[i].at[layer], to, sems.at[i])]
    return copies


def place_quarters(layer, scal, quarters, held, which=range(7)):
    yl, core, odd = scal[0], scal[1], scal[4]
    chunks = CHUNKS[layer]
    for h in range(2):

        @pl.when(odd == h)
        def _():
            for n in range(4):
                core_at = core if n < 2 else 1 - core
                top = pl.ds(pl.multiple_of((1 - yl) * 288 + core_at * 144, 16), 144)
                left = (1 - yl) * 768 + core_at * 384
                for c, (first, last) in enumerate(chunks):
                    ref = quarters[n * len(chunks) + c]
                    for k, (i, row, column, size) in enumerate(QUARTERS[h ^ (n % 2)][first:last]):
                        if i not in which:
                            continue
                        value = ref[9 * k : 9 * k + 9].reshape(144, 128)
                        if i < 6:
                            held[i][top, column : column + size] = value[:, :size]
                        else:
                            held[i][row : row + 144, pl.ds(pl.multiple_of(left + column, 128), 128)] = value


def pack_kernel(layer, first, last, *refs):
    scal, own, packed, regions, sems = split(refs, 1, 7, 1, 7, 1)
    core, odd = scal[1], scal[4]
    for h in range(2):

        @pl.when(odd == h)
        def _():
            blocks = QUARTERS[h][first:last]
            copies = []
            for i in sorted({block[0] for block in blocks}):
                if i < 6:
                    source = own[i].at[layer, pl.ds(pl.multiple_of(core * 144, 16), 144), :]
                else:
                    source = own[i].at[layer, :, pl.ds(pl.multiple_of(core * 384, 128), 384)]
                copies.append(pltpu.make_async_copy(source, regions[i], sems.at[i]))
            for copy in copies:
                copy.start()
            for copy in copies:
                copy.wait()
            for k, (i, row, column, size) in enumerate(blocks):
                value = regions[i][row : row + 144, column : column + size]
                packed[9 * k : 9 * k + 9, :, 0:size] = value.reshape(9, 16, size)


def start_all(copies):
    for group in copies:
        for copy in group:
            copy.start()


def wait_for(copies, *which):
    for i in which:
        for copy in copies[i]:
            copy.wait()


def forward(x, gains, layer, held, copies, cosine, sine, bias, wide, qkv, pt, ot, x1, gate, up, m):
    wq, wk, wv, wo, wg, wu, wd = held
    h1 = (x * factor_of(x) * gains[2 * layer : 2 * layer + 1, :]).astype(BF16)
    wait_for(copies, 0, 1, 2)
    wide[:, 0:576] = dot(h1, wq[...])
    wide[:, 576:768] = dot(h1, wk[...])
    wide[:, 768:960] = dot(h1, wv[...])
    for c in range(6):
        chunk = wide[:, 128 * c : 128 * c + 128]
        qkv[:, 128 * c : 128 * c + 128] = (
            chunk * cosine[...] + swapped_halves(chunk) * sine[...]
        ).astype(BF16)
    qkv[:, 768:960] = wide[:, 768:960].astype(BF16)
    for group in range(3):
        key = qkv[:, 576 + HEAD * group : 576 + HEAD * (group + 1)]
        value = qkv[:, 768 + HEAD * group : 768 + HEAD * (group + 1)]
        scores = dot_nt(key, heads_of(qkv, group)) * SCALE + jnp.concatenate([bias[...]] * 3, axis=1)
        exponent = jnp.exp(scores - jnp.max(scores, axis=0, keepdims=True))
        low = (exponent * (1.0 / jnp.sum(exponent, axis=0, keepdims=True))).astype(BF16)
        pt[group] = low
        mixed = dot_tn(value, low).astype(BF16)
        for n in range(3):
            h = 3 * group + n
            ot[HEAD * h : HEAD * (h + 1), :] = mixed[:, ROWS * n : ROWS * (n + 1)]
    wait_for(copies, 3)
    middle = x + dot(ot[...].T, wo[...])
    x1[...] = middle
    h2 = (middle * factor_of(middle) * gains[2 * layer + 1 : 2 * layer + 2, :]).astype(BF16)
    wait_for(copies, 4, 5, 6)

    def step(i, total):
        at = pl.ds(pl.multiple_of(i * STEP, STEP), STEP)
        gate_part = dot(h2, wg[:, at])
        up_part = dot(h2, wu[:, at])
        gate[:, at] = gate_part
        up[:, at] = up_part
        low = (gate_part * sigmoid(gate_part) * up_part).astype(BF16)
        m[:, at] = low
        return total + dot_nt(low, wd[:, at])

    return lax.fori_loop(0, FF // STEP, step, middle)


def writer(scal, keeps, sends, base):
    def put(t, core_rel, yl_rel, slot, first, value):
        ref = (keeps, sends)[core_rel][t]
        bits = {"y": yl_rel, "x": slot >> 1, "z": slot & 1}
        i, j, k = (bits[name] for name in ORDERS[t])
        ref[i, j, k, 16 * (first - base) : 16 * (first - base) + value.shape[0], :] = value

    def store(value, first, pair):
        low = value.astype(BF16)
        for n in range(2):
            column = 2 * pair + n
            t, j = column // 4, column % 4
            for yl_rel in range(2):
                for core_rel in range(2):
                    at = (yl_rel * 2 + core_rel) * 144
                    piece = low[at : at + 144, 128 * n : 128 * n + 128]
                    put(t, core_rel, yl_rel, j ^ scal[2 + core_rel], first, piece)

    return put, store


def turn(scal, flipped, to_ref):
    yl, core = scal[0], scal[1]
    for yl_at in range(2):
        for core_at in range(2):
            to = ((yl_at ^ yl) * 2 + (core_at ^ core)) * 144
            source = (yl_at * 2 + core_at) * 144
            to_ref[pl.ds(pl.multiple_of(to, 16), 144), :] = flipped[source : source + 144, :]


def backward_mixer(g, f_turned, gains, layer, scal, held, x1, gate, up, m, dgate, dup, h2_turned, put, store):
    wg, wu, wd = held[4:]
    yl, core = scal[0], scal[1]
    gain_two = gains[2 * layer + 1 : 2 * layer + 2, :]
    f = g.astype(BF16)
    middle = x1[...]
    r2 = factor_of(middle)
    n2 = middle * r2
    turn(scal, (n2 * gain_two).astype(BF16).T, h2_turned)

    def step(i, total):
        at = pl.ds(pl.multiple_of(i * STEP, STEP), STEP)
        dm = dot(f, wd[:, at])
        gate_part, up_part = gate[:, at], up[:, at]
        sig = sigmoid(gate_part)
        dg = (dm * up_part * sig * (1.0 + gate_part * (1.0 - sig))).astype(BF16)
        du = (dm * gate_part * sig).astype(BF16)
        dgate[:, at] = dg
        dup[:, at] = du
        return total + dot_nt(dg, wg[:, at]) + dot_nt(du, wu[:, at])

    dh2 = lax.fori_loop(0, FF // STEP, step, jnp.zeros((ROWS, WIDTH), F32))
    mixer_grad = jnp.sum(dh2 * n2, axis=0, keepdims=True)
    e2 = dh2 * gain_two
    g1 = g + r2 * (e2 - n2 * jnp.mean(e2 * n2, axis=-1, keepdims=True))
    for pair in range(6):
        store(dot(h2_turned[...], dgate[:, STEP * pair : STEP * (pair + 1)]), 0, pair)
        store(dot(h2_turned[...], dup[:, STEP * pair : STEP * (pair + 1)]), 9, pair)
    for yl_rel in range(2):
        for t in range(3):
            columns = [
                m[:, pl.ds(pl.multiple_of(((yl_rel ^ yl) * 6 + 2 * t + (core_rel ^ core)) * 128, 128), 128)]
                for core_rel in range(2)
            ]
            low = dot(f_turned[...], jnp.concatenate(columns, axis=1)).astype(BF16)
            for core_rel in range(2):
                for j in range(4):
                    piece = low[144 * j : 144 * j + 144, 128 * core_rel : 128 * core_rel + 128]
                    put(t, core_rel, yl_rel, j ^ scal[2 + core_rel], 18, piece)
    return g1, mixer_grad


def backward_attention(
    g1, mixer_grad, x, gains, layer, scal, held, angles, wide, qkv, pt, ot,
    parts, h1_turned, o_turned, query_t, apad, vectors, put, store,
):
    wq, wk, wv, wo = held[:4]
    cosine, sine, cosine_t, sine_t = angles
    gain_one = gains[2 * layer : 2 * layer + 1, :]
    a = g1.astype(BF16)
    apad[...] = jnp.zeros(apad.shape, BF16)
    apad[:, 64:640] = a
    do = dot_nt(a, wo[...]).astype(BF16)
    parts[...] = jnp.zeros(parts.shape, BF16)
    for group in range(3):
        key = qkv[:, 576 + HEAD * group : 576 + HEAD * (group + 1)]
        value = qkv[:, 768 + HEAD * group : 768 + HEAD * (group + 1)]
        grads = jnp.concatenate(
            [do[:, HEAD * h : HEAD * (h + 1)] for h in range(3 * group, 3 * group + 3)], axis=0
        )
        low = pt[group]
        p = low.astype(F32)
        dp = dot_nt(value, grads)
        ds = (p * (dp - jnp.sum(p * dp, axis=0, keepdims=True))).astype(BF16)
        dq = dot_tn(key, ds) * SCALE
        for n in range(3):
            at = HEAD * (3 * group + n)
            first, second = dq[0:32, ROWS * n : ROWS * (n + 1)], dq[32:64, ROWS * n : ROWS * (n + 1)]
            query_t[at : at + 32, :] = (first * cosine_t[...] + second * sine_t[...]).astype(BF16)
            query_t[at + 32 : at + 64, :] = (second * cosine_t[...] - first * sine_t[...]).astype(BF16)
        wide[:, HEAD * group : HEAD * (group + 1)] = dot(ds, heads_of(qkv, group)) * SCALE
        parts[:, 768 + HEAD * group : 768 + HEAD * (group + 1)] = dot(low, grads).astype(BF16)
    parts[:, 0:576] = query_t[...].T
    for c in range(2):
        chunk = wide[:, 128 * c : 128 * c + 128]
        turned_back = (chunk * cosine[...] - swapped_halves(chunk) * sine[...]).astype(BF16)
        size = 128 - 64 * c
        parts[:, 576 + 128 * c : 576 + 128 * c + size] = turned_back[:, 0:size]
    dh1 = (
        dot_nt(parts[:, 0:576], wq[...])
        + dot_nt(parts[:, 576:768], wk[...])
        + dot_nt(parts[:, 768:960], wv[...])
    )
    r1 = factor_of(x)
    n1 = x * r1
    attend_grad = jnp.sum(dh1 * n1, axis=0, keepdims=True)
    e1 = dh1 * gain_one
    result = g1 + r1 * (e1 - n1 * jnp.mean(e1 * n1, axis=-1, keepdims=True))

    turn(scal, (n1 * gain_one).astype(BF16).T, h1_turned)
    turn(scal, ot[...], o_turned)
    for pair in range(3):
        store(dot(h1_turned[...], parts[:, STEP * pair : STEP * (pair + 1)]), 27, pair)
    mixed_tile = dot(h1_turned[...], parts[:, 768:1024])
    columns = jnp.concatenate([jnp.zeros((WIDTH, 128), F32), dot(o_turned[...], apad[:, 0:128])], axis=1)
    store(mixed_tile + columns, 27, 3)
    for pair in range(4, 6):
        at = 128 + STEP * (pair - 4)
        store(dot(o_turned[...], apad[:, at : at + STEP]), 27, pair)

    vectors[...] = jnp.zeros(vectors.shape, F32)
    for c in range(5):
        size = min(128, WIDTH - 128 * c)
        vectors[c : c + 1, 0:size] = attend_grad[:, 128 * c : 128 * c + size]
        vectors[c + 5 : c + 6, 0:size] = mixer_grad[:, 128 * c : 128 * c + size]
    tile = jnp.concatenate([vectors[...], jnp.zeros((16, 128), F32)], axis=0).astype(BF16)
    for core_rel in range(2):
        for yl_rel in range(2):
            for slot in range(4):
                put(0, core_rel, yl_rel, slot, 36, tile)
    return result


def split(refs, *counts):
    out, at = [], 0
    for count in counts:
        out.append(refs[at] if count == 1 else refs[at : at + count])
        at += count
    return out


def first_kernel(*refs):
    scal, x, gains, cosine, sine, bias, quarters, own, x_out, qkv, pt, ot, x1, gate, up, m, wide, held, sems = split(
        refs, 1, 1, 1, 1, 1, 1, 4, 7, 1, 1, 1, 1, 1, 1, 1, 1, 1, 7, 1
    )
    copies = weight_copies(0, scal, own, held, sems)
    start_all(copies)
    place_quarters(0, scal, quarters, held)
    x_out[...] = forward(
        x[...].T.astype(F32), gains, 0, held, copies, cosine, sine, bias, wide, qkv, pt, ot, x1, gate, up, m
    )


def second_kernel(*refs):
    (
        scal, x, cotangent, gains, angles, bias, quarters, own, result, g_out, keeps, sends,
        qkv, pt, ot, x1, gate, up, m, dgate, dup, h2_turned,
        parts, h1_turned, o_turned, query_t, apad, vectors, wide, held, sems,
    ) = split(
        refs, 1, 1, 1, 1, 4, 1, 4, 7, 1, 1, 3, 3,
        1, 1, 1, 1, 1, 1, 1, 1, 1, 1,
        1, 1, 1, 1, 1, 1, 1, 7, 1,
    )
    copies = weight_copies(1, scal, own, held, sems)
    start_all(copies)
    place_quarters(1, scal, quarters, held)
    done = forward(
        x[...], gains, 1, held, copies, angles[0], angles[1], bias, wide, qkv, pt, ot, x1, gate, up, m
    )
    result[...] = done.astype(BF16).T
    put, store = writer(scal, keeps, sends, 0)
    g1, mixer_grad = backward_mixer(
        cotangent[...].T.astype(F32), cotangent, gains, 1, scal, held, x1, gate, up, m, dgate, dup, h2_turned,
        put, store,
    )
    g_out[...] = backward_attention(
        g1, mixer_grad, x[...], gains, 1, scal, held, angles, wide, qkv, pt, ot,
        parts, h1_turned, o_turned, query_t, apad, vectors, put, store,
    )


def third_kernel(*refs):
    (
        scal, x, g, gains, angles, quarters, qkv, pt, ot, x1, gate, up, m, own, g_out, keeps, sends,
        dgate, dup, h2_turned, f_turned, parts, h1_turned, o_turned, query_t, apad, vectors, wide, held, sems,
    ) = split(
        refs, 1, 1, 1, 1, 4, 4, 1, 1, 1, 1, 1, 1, 1, 7, 1, 3, 3,
        1, 1, 1, 1, 1, 1, 1, 1, 1, 1, 1, 7, 1,
    )
    copies = weight_copies(0, scal, own, held, sems)
    start_all(copies)
    place_quarters(0, scal, quarters, held)
    f_turned[...] = g[...].astype(BF16).T
    wait_for(copies, 0, 1, 2, 3, 4, 5, 6)
    put, store = writer(scal, keeps, sends, 0)
    g1, mixer_grad = backward_mixer(
        g[...], f_turned, gains, 0, scal, held, x1, gate, up, m, dgate, dup, h2_turned, put, store
    )
    done = backward_attention(
        g1, mixer_grad, x[...].T.astype(F32), gains, 0, scal, held, angles, wide, qkv, pt, ot,
        parts, h1_turned, o_turned, query_t, apad, vectors, put, store,
    )
    g_out[...] = done.T


def last_kernel(*refs):
    scal, sources, attend, query, key, value, output, mixer, gate, up, down, wide, rows = split(
        refs, 1, 8, 1, 1, 1, 1, 1, 1, 1, 1, 1, 1, 1
    )
    yl, core = scal[0], scal[1]
    for layer in range(2):

        @pl.when(pl.program_id(0) == layer)
        def _():
            tiles = [jnp.zeros((16, 128), F32)] * 2
            for core_rel in range(2):
                core_at = core ^ core_rel
                at = pl.ds(pl.multiple_of(core_at * 144, 16), 144)
                for slot in range(4):
                    source = sources[4 * layer + 2 * core_rel + slot // 2].at[slot % 2]
                    relative = slot if layer == 0 else (slot % 2) * 2 + slot // 2
                    j = relative ^ scal[2 + core_rel]
                    for t in range(3):
                        base = sum(TILES[:t])
                        lanes = pl.ds(pl.multiple_of((4 * t + j) * 128, 128), 128)
                        gate[0, at, lanes] = source[16 * base : 16 * base + 144, :].astype(F32)
                        up[0, at, lanes] = source[16 * base + 144 : 16 * base + 288, :].astype(F32)
                        wide[at, lanes] = source[16 * base + 432 : 16 * base + 576, :].astype(F32)
                        to = pl.ds(pl.multiple_of((2 * t + core_at) * 128, 128), 128)
                        down[0, pl.ds(pl.multiple_of(144 * j, 16), 144), to] = (
                            source[16 * base + 288 : 16 * base + 432, :].astype(F32)
                        )
                    tiles[core_rel] = jnp.where(j == 0, source[576:592, :].astype(F32), tiles[core_rel])
            query[0] = wide[:, 0:576]
            key[0] = wide[:, 576:768]
            value[0] = wide[:, 768:960]
            output[0] = wide[:, 960:1536]
            tile = jnp.where(core == 0, tiles[0], tiles[1])
            for c in range(5):
                size = min(128, WIDTH - 128 * c)
                rows[0:1, 128 * c : 128 * c + size] = tile[c : c + 1, 0:size]
                rows[1:2, 128 * c : 128 * c + size] = tile[c + 5 : c + 6, 0:size]
            share = jnp.where(yl == 0, rows[:, 0:288], rows[:, 288:576])
            attend[0] = share[0:1, :]
            mixer[0] = share[1:2, :]


SMEM = pl.BlockSpec(memory_space=pltpu.SMEM)
VMEM = pl.BlockSpec(memory_space=pltpu.VMEM)
HBM = pl.BlockSpec(memory_space=pl.ANY)
PARAMS = pltpu.CompilerParams(vmem_limit_bytes=VMEM_LIMIT)

FORWARD_STATE = (
    ((ROWS, 1024), BF16),
    ((3, ROWS, 3 * ROWS), BF16),
    ((WIDTH, ROWS), BF16),
    ((ROWS, WIDTH), F32),
    ((ROWS, FF), F32),
    ((ROWS, FF), F32),
    ((ROWS, FF), BF16),
)
MIXER_SCRATCH = [
    pltpu.VMEM((ROWS, FF), BF16),
    pltpu.VMEM((ROWS, FF), BF16),
    pltpu.VMEM((WIDTH, ROWS), BF16),
]
ATTENTION_SCRATCH = [
    pltpu.VMEM((ROWS, 1024), BF16),
    *[pltpu.VMEM((WIDTH, ROWS), BF16)] * 3,
    pltpu.VMEM((ROWS, 640), BF16),
    pltpu.VMEM((16, 128), F32),
]
WIDE = [pltpu.VMEM((ROWS, 1024), F32)]


def held_scratch(which=range(7)):
    return [pltpu.VMEM(WEIGHT_SHAPES[i], BF16) for i in which] + [pltpu.SemaphoreType.DMA((7,))]


def packed(*tiles):
    return [out((2, 2, 2, 16 * count, 128), BF16) for count in tiles * 2]


def out(shape, kind):
    return jax.ShapeDtypeStruct(shape, kind)


def cost(gflop, mbytes):
    return pl.CostEstimate(flops=int(gflop * 1e9), bytes_accessed=int(mbytes * 1e6), transcendentals=0)


def call_pack(layer, first, last, scal, own):
    return pl.pallas_call(
        functools.partial(pack_kernel, layer, first, last),
        out_shape=out((9 * (last - first), 16, 128), BF16),
        in_specs=[SMEM] + [HBM] * 7,
        out_specs=VMEM,
        scratch_shapes=[
            *[pltpu.VMEM((144, WEIGHT_SHAPES[i][1]), BF16) for i in range(6)],
            pltpu.VMEM((576, 384), BF16),
            pltpu.SemaphoreType.DMA((7,)),
        ],
        compiler_params=pltpu.CompilerParams(vmem_limit_bytes=PACK_VMEM),
        cost_estimate=cost(0, 4),
        name="pack",
    )(scal, *own)


def call_first(scal, x, gains, cosine, sine, bias, quarters, own):
    return pl.pallas_call(
        first_kernel,
        out_shape=[out((ROWS, WIDTH), F32)] + [out(*state) for state in FORWARD_STATE],
        in_specs=[SMEM] + [VMEM] * 9 + [HBM] * 7,
        out_specs=[VMEM] * 8,
        scratch_shapes=WIDE + held_scratch(),
        compiler_params=PARAMS,
        cost_estimate=cost(2.2, 16),
        name="first_forward",
    )(scal, x, gains, cosine, sine, bias, *quarters, *own)


def call_second(scal, x, cotangent, gains, angles, bias, quarters, own):
    return pl.pallas_call(
        second_kernel,
        out_shape=[out((WIDTH, ROWS), BF16), out((ROWS, WIDTH), F32)] + packed(*TILES),
        in_specs=[SMEM] + [VMEM] * 12 + [HBM] * 7,
        out_specs=[VMEM] * 8,
        scratch_shapes=[pltpu.VMEM(*state) for state in FORWARD_STATE]
        + MIXER_SCRATCH
        + ATTENTION_SCRATCH
        + WIDE
        + held_scratch(),
        compiler_params=PARAMS,
        cost_estimate=cost(7, 18),
        name="second_both",
    )(scal, x, cotangent, gains, *angles, bias, *quarters, *own)


def call_third(scal, x, g, gains, angles, quarters, states, own):
    return pl.pallas_call(
        third_kernel,
        out_shape=[out((WIDTH, ROWS), F32)] + packed(*TILES),
        in_specs=[SMEM] + [VMEM] * 18 + [HBM] * 7,
        out_specs=[VMEM] * 7,
        scratch_shapes=MIXER_SCRATCH
        + [pltpu.VMEM((WIDTH, ROWS), BF16)]
        + ATTENTION_SCRATCH
        + WIDE
        + held_scratch(),
        compiler_params=PARAMS,
        cost_estimate=cost(5, 22),
        name="first_backward",
    )(scal, x, g, gains, *angles, *quarters, *states, *own)


def call_last(scal, sources):
    shapes = [(1, 288), (288, 576), (288, 192), (288, 192), (288, 576), (1, 288)]
    shapes += [(288, 1536), (288, 1536), (576, 768)]
    return pl.pallas_call(
        last_kernel,
        grid=(2,),
        out_shape=[out((2, *s), F32) for s in shapes],
        in_specs=[SMEM] + [pl.BlockSpec((2, 16 * sum(TILES), 128), lambda layer: (0, 0, 0))] * 8,
        out_specs=[pl.BlockSpec((1, *s), lambda layer: (layer, 0, 0)) for s in shapes],
        scratch_shapes=[pltpu.VMEM((288, FF), F32), pltpu.VMEM((2, WIDTH), F32)],
        compiler_params=LATE,
        cost_estimate=cost(0.1, 22),
        name="unpack",
    )(scal, *sources)


def tables(row):
    index = jnp.arange(ROWS, dtype=jnp.int32)
    fresh = jnp.concatenate([jnp.ones((1,), dtype=bool), row[1:] != row[:-1]])
    starts = lax.cummax(jnp.where(fresh, index, 0), axis=0)
    positions = (index - starts).astype(F32)
    frequency = ROPE_BASE ** (-(jnp.arange(HEAD // 2, dtype=F32) * 2.0 / HEAD))
    angles = positions[:, None] * frequency[None, :]
    cosine, sine = jnp.cos(angles), jnp.sin(angles)
    allowed = (row[:, None] == row[None, :]) & (index[:, None] <= index[None, :])
    bias = jnp.where(allowed, 0.0, MASKED).astype(F32)
    wide_sine = jnp.tile(jnp.concatenate([-sine, sine], axis=1), (1, 2))
    return (jnp.tile(cosine, (1, 4)), wide_sine, cosine.T, sine.T), bias


def ring_bits(at):
    high = at // 2
    return high ^ (at % 2), high


def halved(t, keeps, cames):
    def both(n):
        return jnp.concatenate([k[t][n] + c[t][n] for k, c in zip(keeps, cames)], axis=-2)

    total = both(0) + swap(both(1), STEPS[t][0])
    total = total[0] + swap(total[1], STEPS[t][1])
    return total[0] + swap(total[1], STEPS[t][2])


def summed(total, bits):
    code = 2 * bits["xv"] + bits["zv"]
    rows = total.shape[0] // 4

    def quarter(n):
        return lax.dynamic_slice_in_dim(total, (code ^ n) * rows, rows)

    came = [swap(quarter(n), move) for n, move in ((1, "zv"), (2, "xv"), (3, "xzv"))]
    mine = sum((a.astype(F32) for a in came), quarter(0).astype(F32)).astype(BF16)
    mine = mine + swap(mine, "yh")
    parts = [mine] + [swap(mine, move) for move in ("zv", "xv", "xzv")]
    low, high = bits["zv"] == 0, bits["xv"] == 0
    parts = [jnp.where(low, parts[n], parts[n ^ 1]) for n in range(4)]
    return jnp.concatenate([jnp.where(high, parts[n], parts[n ^ 2]) for n in range(4)])


def gathered(total, first, second):
    total = jnp.stack([total, swap(total, first)])
    far = swap(total, second)
    return total, far, swap(total, "core"), swap(far, "core")


def local(
    activations, seg_ids, cotangent, attend_gain, query_weight, key_matrix, value_matrix, output_weight,
    mixer_gain, gate_weight, up_weight, down_weight,
):
    z, yh, x, core, yl = (lax.axis_index(name) for name in ALL)
    (x_low, x_high), (z_low, z_high) = ring_bits(x), ring_bits(z)
    bits = {
        "xu": jnp.where(core == 0, x_low, x_high),
        "xv": jnp.where(core == 0, x_high, x_low),
        "zu": jnp.where(core == 0, z_low, z_high),
        "zv": jnp.where(core == 0, z_high, z_low),
    }
    scal = jnp.stack(
        [yl, core, 2 * bits["xu"] + bits["zu"], 2 * bits["xv"] + bits["zv"], x % 2]
    ).astype(jnp.int32)
    own = (
        query_weight, key_matrix, value_matrix, output_weight, gate_weight, up_weight,
        jnp.swapaxes(down_weight, 1, 2),
    )
    straight = [swap(call_pack(layer, *CHUNKS[layer][0], scal, own), "y") for layer in range(2)]
    gain_share = jnp.stack([attend_gain[0], mixer_gain[0], attend_gain[1], mixer_gain[1]])
    gain_other = swap(gain_share, "y")
    gains = jnp.where(
        yl == 0,
        jnp.concatenate([gain_share, gain_other], axis=1),
        jnp.concatenate([gain_other, gain_share], axis=1),
    ).astype(F32)
    angles, bias = tables(seg_ids[0])
    across = [swap(a, "xu") for a in straight]
    quarters_0 = (straight[0], across[0], swap(straight[0], "core"), swap(across[0], "core"))
    sibling_1 = swap(straight[1], "core")
    scal_first, sibling_1 = lax.optimization_barrier((scal, sibling_1))
    x_1, *states = call_first(scal_first, activations.T, gains, angles[0], angles[1], bias, quarters_0, own)
    x_1, across_1 = lax.optimization_barrier((x_1, across[1]))
    quarters_1 = (straight[1], across_1, sibling_1, swap(across_1, "core"))
    result, g, *packed_1 = call_second(scal, x_1, cotangent.T, gains, angles, bias, quarters_1, own)
    came_1 = [swap(a, "core") for a in packed_1[3:]]
    input_grad, *packed_0 = call_third(scal, activations.T, g, gains, angles, quarters_0, states, own)
    sends = lax.optimization_barrier((*packed_0[3:], *came_1))
    came_0, came_1 = [swap(a, "core") for a in sends[:3]], sends[3:]
    parts = [halved(t, (packed_0, packed_1), (came_0, came_1)) for t in range(3)]
    layers = [a[: 16 * TILES[t]] for t, a in enumerate(parts)] + [a[16 * TILES[t] :] for t, a in enumerate(parts)]
    total = summed(jnp.concatenate(layers), bits)
    half = total.shape[0] // 2
    sources = [*gathered(total[:half], "zu", "xu"), *gathered(total[half:], "xu", "zu")]
    grads = list(call_last(scal, sources))
    grads[0], grads[5] = grads[0][:, 0], grads[5][:, 0]
    grads[8] = jnp.swapaxes(grads[8], 1, 2)
    return (result.T, input_grad.T, *grads)


def solution(mesh):
    fine = jax.sharding.Mesh(mesh.devices.reshape(SIZES), ALL)
    token, own = P(ALL, None), P(None, "yl")
    matrix = P(None, "yl", None)
    in_specs = (token, token, token, own, matrix, matrix, matrix, matrix, own, matrix, matrix, matrix)
    out_specs = (token, token, own, matrix, matrix, matrix, matrix, own, matrix, matrix, matrix)
    return jax.shard_map(local, mesh=fine, in_specs=in_specs, out_specs=out_specs, check_vma=False)
```

```python
import functools

import jax
import jax.numpy as jnp
from jax import lax
from jax.experimental import pallas as pl
from jax.experimental.pallas import tpu as pltpu
from jax.sharding import PartitionSpec as P

F32 = jnp.float32
BF16 = jnp.bfloat16
ROWS = 256
WIDTH = 576
FF = 1536
HEAD = 64
EPSILON = 1e-05
ROPE_BASE = 100000.0
MASKED = -1e30
SCALE = HEAD**-0.5
STEP = 256

ALL = ("z", "yh", "x", "core", "yl")
SIZES = (4, 2, 4, 2, 2)
WEIGHT_SHAPES = ((576, 576), (576, 192), (576, 192), (576, 576), (576, 1536), (576, 1536), (576, 1536))
TILES = (38, 36, 36)
BLOCKS = [(i, 0, c, min(128, WEIGHT_SHAPES[i][1] - c)) for i in range(6) for c in range(0, WEIGHT_SHAPES[i][1], 128)]
BLOCKS += [(6, r, c, 128) for r in range(0, 576, 144) for c in range(0, 384, 128)]
QUARTERS = (BLOCKS[:25], BLOCKS[25:])
CHUNKS = (((0, 25),), ((0, 25),))
VMEM_LIMIT = 50 * 2**20
LAST_VMEM = 30 * 2**20
LATE = pltpu.CompilerParams(vmem_limit_bytes=LAST_VMEM)

PACK_VMEM = 60 * 2**20
ORDERS = (("y", "x", "z"), ("z", "y", "x"), ("x", "z", "y"))
STEPS = (("y", "xu", "zu"), ("zu", "y", "xu"), ("xu", "zu", "y"))


def coordinates(index):
    out = []
    for size in reversed(SIZES):
        out.append(index % size)
        index //= size
    return tuple(reversed(out))


def place(z, yh, x, core, yl):
    return (((z * 2 + yh) * 4 + x) * 2 + core) * 2 + yl


def move_y(z, yh, x, core, yl):
    y = yh * 2 + yl
    y = y ^ 1 if core == 0 else 3 - y
    return (z, y // 2, x, core, y % 2)


def move_yh(z, yh, x, core, yl):
    return (z, 1 - yh, x, core, yl)


def move_core(z, yh, x, core, yl):
    return (z, yh, x, 1 - core, yl)


def ring_step(at, low):
    return at ^ 1 if low else 3 - at


def move_x(first, z, yh, x, core, yl):
    return (z, yh, ring_step(x, first == (core == 0)), core, yl)


def move_z(first, z, yh, x, core, yl):
    return (ring_step(z, first == (core == 0)), yh, x, core, yl)


MOVES = {
    "y": move_y,
    "yh": move_yh,
    "core": move_core,
    "xu": functools.partial(move_x, True),
    "xv": functools.partial(move_x, False),
    "zu": functools.partial(move_z, True),
    "zv": functools.partial(move_z, False),
    "xzv": lambda *at: move_x(False, *move_z(False, *at)),
}


def swap(a, move):
    return lax.ppermute(a, ALL, [(i, place(*MOVES[move](*coordinates(i)))) for i in range(128)])


def dot(a, b):
    return lax.dot_general(a, b, (((1,), (0,)), ((), ())), preferred_element_type=F32)


def dot_nt(a, b):
    return lax.dot_general(a, b, (((1,), (1,)), ((), ())), preferred_element_type=F32)


def dot_tn(a, b):
    return lax.dot_general(a, b, (((0,), (0,)), ((), ())), preferred_element_type=F32)


def factor_of(x):
    return lax.rsqrt(jnp.mean(x * x, axis=-1, keepdims=True) + EPSILON)


def sigmoid(u):
    return 0.5 * jnp.tanh(0.5 * u) + 0.5


def swapped_halves(chunk):
    lane = lax.broadcasted_iota(jnp.int32, chunk.shape, 1)
    return jnp.where(lane % HEAD < HEAD // 2, pltpu.roll(chunk, 96, 1), pltpu.roll(chunk, 32, 1))


def heads_of(ref, group):
    return jnp.concatenate([ref[:, HEAD * h : HEAD * (h + 1)] for h in range(3 * group, 3 * group + 3)], axis=0)


def weight_copies(layer, scal, own, held, sems, which=range(7)):
    yl = scal[0]
    copies = [[] for _ in range(7)]
    for i in which:
        if i < 6:
            to = held[i].at[pl.ds(pl.multiple_of(yl * 288, 16), 288), :]
        else:
            to = held[i].at[:, pl.ds(pl.multiple_of(yl * 768, 128), 768)]
        copies[i] = [pltpu.make_async_copy(own[i].at[layer], to, sems.at[i])]
    return copies


def place_quarters(layer, scal, quarters, held, which=range(7)):
    yl, core, odd = scal[0], scal[1], scal[4]
    chunks = CHUNKS[layer]
    for h in range(2):

        @pl.when(odd == h)
        def _():
            for n in range(4):
                core_at = core if n < 2 else 1 - core
                top = pl.ds(pl.multiple_of((1 - yl) * 288 + core_at * 144, 16), 144)
                left = (1 - yl) * 768 + core_at * 384
                for c, (first, last) in enumerate(chunks):
                    ref = quarters[n * len(chunks) + c]
                    for k, (i, row, column, size) in enumerate(QUARTERS[h ^ (n % 2)][first:last]):
                        if i not in which:
                            continue
                        value = ref[9 * k : 9 * k + 9].reshape(144, 128)
                        if i < 6:
                            held[i][top, column : column + size] = value[:, :size]
                        else:
                            held[i][row : row + 144, pl.ds(pl.multiple_of(left + column, 128), 128)] = value


def pack_kernel(layer, first, last, *refs):
    scal, own, packed, regions, sems = split(refs, 1, 7, 1, 7, 1)
    core, odd = scal[1], scal[4]
    for h in range(2):

        @pl.when(odd == h)
        def _():
            blocks = QUARTERS[h][first:last]
            copies = []
            for i in sorted({block[0] for block in blocks}):
                if i < 6:
                    source = own[i].at[layer, pl.ds(pl.multiple_of(core * 144, 16), 144), :]
                else:
                    source = own[i].at[layer, :, pl.ds(pl.multiple_of(core * 384, 128), 384)]
                copies.append(pltpu.make_async_copy(source, regions[i], sems.at[i]))
            for copy in copies:
                copy.start()
            for copy in copies:
                copy.wait()
            for k, (i, row, column, size) in enumerate(blocks):
                value = regions[i][row : row + 144, column : column + size]
                packed[9 * k : 9 * k + 9, :, 0:size] = value.reshape(9, 16, size)


def start_all(copies):
    for group in copies:
        for copy in group:
            copy.start()


def wait_for(copies, *which):
    for i in which:
        for copy in copies[i]:
            copy.wait()


def forward(x, gains, layer, held, copies, cosine, sine, bias, wide, qkv, pt, ot, x1, gate, up, m):
    wq, wk, wv, wo, wg, wu, wd = held
    h1 = (x * factor_of(x) * gains[2 * layer : 2 * layer + 1, :]).astype(BF16)
    wait_for(copies, 0, 1, 2)
    wide[:, 0:576] = dot(h1, wq[...])
    wide[:, 576:768] = dot(h1, wk[...])
    wide[:, 768:960] = dot(h1, wv[...])
    for c in range(6):
        chunk = wide[:, 128 * c : 128 * c + 128]
        qkv[:, 128 * c : 128 * c + 128] = (
            chunk * cosine[...] + swapped_halves(chunk) * sine[...]
        ).astype(BF16)
    qkv[:, 768:960] = wide[:, 768:960].astype(BF16)
    for group in range(3):
        key = qkv[:, 576 + HEAD * group : 576 + HEAD * (group + 1)]
        value = qkv[:, 768 + HEAD * group : 768 + HEAD * (group + 1)]
        scores = dot_nt(key, heads_of(qkv, group)) * SCALE + jnp.concatenate([bias[...]] * 3, axis=1)
        exponent = jnp.exp(scores - jnp.max(scores, axis=0, keepdims=True))
        low = (exponent * (1.0 / jnp.sum(exponent, axis=0, keepdims=True))).astype(BF16)
        pt[group] = low
        mixed = dot_tn(value, low).astype(BF16)
        for n in range(3):
            h = 3 * group + n
            ot[HEAD * h : HEAD * (h + 1), :] = mixed[:, ROWS * n : ROWS * (n + 1)]
    wait_for(copies, 3)
    middle = x + dot(ot[...].T, wo[...])
    x1[...] = middle
    h2 = (middle * factor_of(middle) * gains[2 * layer + 1 : 2 * layer + 2, :]).astype(BF16)
    wait_for(copies, 4, 5, 6)

    def step(i, total):
        at = pl.ds(pl.multiple_of(i * STEP, STEP), STEP)
        gate_part = dot(h2, wg[:, at])
        up_part = dot(h2, wu[:, at])
        gate[:, at] = gate_part.astype(BF16)
        up[:, at] = up_part.astype(BF16)
        low = (gate_part * sigmoid(gate_part) * up_part).astype(BF16)
        m[:, at] = low
        return total + dot_nt(low, wd[:, at])

    return lax.fori_loop(0, FF // STEP, step, middle)


def writer(scal, keeps, sends, base):
    def put(t, core_rel, yl_rel, slot, first, value):
        ref = (keeps, sends)[core_rel][t]
        bits = {"y": yl_rel, "x": slot >> 1, "z": slot & 1}
        i, j, k = (bits[name] for name in ORDERS[t])
        ref[i, j, k, 16 * (first - base) : 16 * (first - base) + value.shape[0], :] = value

    def store(value, first, pair):
        low = value.astype(BF16)
        for n in range(2):
            column = 2 * pair + n
            t, j = column // 4, column % 4
            for yl_rel in range(2):
                for core_rel in range(2):
                    at = (yl_rel * 2 + core_rel) * 144
                    piece = low[at : at + 144, 128 * n : 128 * n + 128]
                    put(t, core_rel, yl_rel, j ^ scal[2 + core_rel], first, piece)

    return put, store


def turn(scal, flipped, to_ref):
    yl, core = scal[0], scal[1]
    for yl_at in range(2):
        for core_at in range(2):
            to = ((yl_at ^ yl) * 2 + (core_at ^ core)) * 144
            source = (yl_at * 2 + core_at) * 144
            to_ref[pl.ds(pl.multiple_of(to, 16), 144), :] = flipped[source : source + 144, :]


def backward_mixer(g, f_turned, gains, layer, scal, held, x1, gate, up, m, dgate, dup, h2_turned, put, store):
    wg, wu, wd = held[4:]
    yl, core = scal[0], scal[1]
    gain_two = gains[2 * layer + 1 : 2 * layer + 2, :]
    f = g.astype(BF16)
    middle = x1[...]
    r2 = factor_of(middle)
    n2 = middle * r2
    turn(scal, (n2 * gain_two).astype(BF16).T, h2_turned)

    def step(i, total):
        at = pl.ds(pl.multiple_of(i * STEP, STEP), STEP)
        dm = dot(f, wd[:, at])
        gate_part, up_part = gate[:, at].astype(F32), up[:, at].astype(F32)
        sig = sigmoid(gate_part)
        dg = (dm * up_part * sig * (1.0 + gate_part * (1.0 - sig))).astype(BF16)
        du = (dm * gate_part * sig).astype(BF16)
        dgate[:, at] = dg
        dup[:, at] = du
        return total + dot_nt(dg, wg[:, at]) + dot_nt(du, wu[:, at])

    dh2 = lax.fori_loop(0, FF // STEP, step, jnp.zeros((ROWS, WIDTH), F32))
    mixer_grad = jnp.sum(dh2 * n2, axis=0, keepdims=True)
    e2 = dh2 * gain_two
    g1 = g + r2 * (e2 - n2 * jnp.mean(e2 * n2, axis=-1, keepdims=True))
    for pair in range(6):
        store(dot(h2_turned[...], dgate[:, STEP * pair : STEP * (pair + 1)]), 0, pair)
        store(dot(h2_turned[...], dup[:, STEP * pair : STEP * (pair + 1)]), 9, pair)
    for yl_rel in range(2):
        for t in range(3):
            columns = [
                m[:, pl.ds(pl.multiple_of(((yl_rel ^ yl) * 6 + 2 * t + (core_rel ^ core)) * 128, 128), 128)]
                for core_rel in range(2)
            ]
            low = dot(f_turned[...], jnp.concatenate(columns, axis=1)).astype(BF16)
            for core_rel in range(2):
                for j in range(4):
                    piece = low[144 * j : 144 * j + 144, 128 * core_rel : 128 * core_rel + 128]
                    put(t, core_rel, yl_rel, j ^ scal[2 + core_rel], 18, piece)
    return g1, mixer_grad


def backward_attention(
    g1, mixer_grad, x, gains, layer, scal, held, angles, wide, qkv, pt, ot,
    parts, h1_turned, o_turned, query_t, apad, vectors, put, store,
):
    wq, wk, wv, wo = held[:4]
    cosine, sine, cosine_t, sine_t = angles
    gain_one = gains[2 * layer : 2 * layer + 1, :]
    a = g1.astype(BF16)
    apad[...] = jnp.zeros(apad.shape, BF16)
    apad[:, 64:640] = a
    do = dot_nt(a, wo[...]).astype(BF16)
    parts[...] = jnp.zeros(parts.shape, BF16)
    for group in range(3):
        key = qkv[:, 576 + HEAD * group : 576 + HEAD * (group + 1)]
        value = qkv[:, 768 + HEAD * group : 768 + HEAD * (group + 1)]
        grads = jnp.concatenate(
            [do[:, HEAD * h : HEAD * (h + 1)] for h in range(3 * group, 3 * group + 3)], axis=0
        )
        low = pt[group]
        p = low.astype(F32)
        dp = dot_nt(value, grads)
        ds = (p * (dp - jnp.sum(p * dp, axis=0, keepdims=True))).astype(BF16)
        dq = dot_tn(key, ds) * SCALE
        for n in range(3):
            at = HEAD * (3 * group + n)
            first, second = dq[0:32, ROWS * n : ROWS * (n + 1)], dq[32:64, ROWS * n : ROWS * (n + 1)]
            query_t[at : at + 32, :] = (first * cosine_t[...] + second * sine_t[...]).astype(BF16)
            query_t[at + 32 : at + 64, :] = (second * cosine_t[...] - first * sine_t[...]).astype(BF16)
        wide[:, HEAD * group : HEAD * (group + 1)] = dot(ds, heads_of(qkv, group)) * SCALE
        parts[:, 768 + HEAD * group : 768 + HEAD * (group + 1)] = dot(low, grads).astype(BF16)
    parts[:, 0:576] = query_t[...].T
    for c in range(2):
        chunk = wide[:, 128 * c : 128 * c + 128]
        turned_back = (chunk * cosine[...] - swapped_halves(chunk) * sine[...]).astype(BF16)
        size = 128 - 64 * c
        parts[:, 576 + 128 * c : 576 + 128 * c + size] = turned_back[:, 0:size]
    dh1 = (
        dot_nt(parts[:, 0:576], wq[...])
        + dot_nt(parts[:, 576:768], wk[...])
        + dot_nt(parts[:, 768:960], wv[...])
    )
    r1 = factor_of(x)
    n1 = x * r1
    attend_grad = jnp.sum(dh1 * n1, axis=0, keepdims=True)
    e1 = dh1 * gain_one
    result = g1 + r1 * (e1 - n1 * jnp.mean(e1 * n1, axis=-1, keepdims=True))

    turn(scal, (n1 * gain_one).astype(BF16).T, h1_turned)
    turn(scal, ot[...], o_turned)
    for pair in range(3):
        store(dot(h1_turned[...], parts[:, STEP * pair : STEP * (pair + 1)]), 27, pair)
    mixed_tile = dot(h1_turned[...], parts[:, 768:1024])
    columns = jnp.concatenate([jnp.zeros((WIDTH, 128), F32), dot(o_turned[...], apad[:, 0:128])], axis=1)
    store(mixed_tile + columns, 27, 3)
    for pair in range(4, 6):
        at = 128 + STEP * (pair - 4)
        store(dot(o_turned[...], apad[:, at : at + STEP]), 27, pair)

    vectors[...] = jnp.zeros(vectors.shape, F32)
    for c in range(5):
        size = min(128, WIDTH - 128 * c)
        vectors[c : c + 1, 0:size] = attend_grad[:, 128 * c : 128 * c + size]
        vectors[c + 5 : c + 6, 0:size] = mixer_grad[:, 128 * c : 128 * c + size]
    tile = jnp.concatenate([vectors[...], jnp.zeros((16, 128), F32)], axis=0).astype(BF16)
    for core_rel in range(2):
        for yl_rel in range(2):
            for slot in range(4):
                put(0, core_rel, yl_rel, slot, 36, tile)
    return result


def split(refs, *counts):
    out, at = [], 0
    for count in counts:
        out.append(refs[at] if count == 1 else refs[at : at + count])
        at += count
    return out


def first_kernel(*refs):
    scal, x, gains, cosine, sine, bias, quarters, own, x_out, qkv, pt, ot, x1, gate, up, m, wide, held, sems = split(
        refs, 1, 1, 1, 1, 1, 1, 4, 7, 1, 1, 1, 1, 1, 1, 1, 1, 1, 7, 1
    )
    copies = weight_copies(0, scal, own, held, sems)
    start_all(copies)
    place_quarters(0, scal, quarters, held)
    x_out[...] = forward(
        x[...].T.astype(F32), gains, 0, held, copies, cosine, sine, bias, wide, qkv, pt, ot, x1, gate, up, m
    )


def second_kernel(*refs):
    (
        scal, x, cotangent, gains, angles, bias, quarters, own, result, g_out, keeps, sends,
        qkv, pt, ot, x1, gate, up, m, dgate, dup, h2_turned,
        parts, h1_turned, o_turned, query_t, apad, vectors, wide, held, sems,
    ) = split(
        refs, 1, 1, 1, 1, 4, 1, 4, 7, 1, 1, 3, 3,
        1, 1, 1, 1, 1, 1, 1, 1, 1, 1,
        1, 1, 1, 1, 1, 1, 1, 7, 1,
    )
    copies = weight_copies(1, scal, own, held, sems)
    start_all(copies)
    place_quarters(1, scal, quarters, held)
    done = forward(
        x[...], gains, 1, held, copies, angles[0], angles[1], bias, wide, qkv, pt, ot, x1, gate, up, m
    )
    result[...] = done.astype(BF16).T
    put, store = writer(scal, keeps, sends, 0)
    g1, mixer_grad = backward_mixer(
        cotangent[...].T.astype(F32), cotangent, gains, 1, scal, held, x1, gate, up, m, dgate, dup, h2_turned,
        put, store,
    )
    g_out[...] = backward_attention(
        g1, mixer_grad, x[...], gains, 1, scal, held, angles, wide, qkv, pt, ot,
        parts, h1_turned, o_turned, query_t, apad, vectors, put, store,
    )


def third_kernel(*refs):
    (
        scal, x, g, gains, angles, quarters, qkv, pt, ot, x1, gate, up, m, own, g_out, keeps, sends,
        dgate, dup, h2_turned, f_turned, parts, h1_turned, o_turned, query_t, apad, vectors, wide, held, sems,
    ) = split(
        refs, 1, 1, 1, 1, 4, 4, 1, 1, 1, 1, 1, 1, 1, 7, 1, 3, 3,
        1, 1, 1, 1, 1, 1, 1, 1, 1, 1, 1, 7, 1,
    )
    copies = weight_copies(0, scal, own, held, sems)
    start_all(copies)
    place_quarters(0, scal, quarters, held)
    f_turned[...] = g[...].astype(BF16).T
    wait_for(copies, 0, 1, 2, 3, 4, 5, 6)
    put, store = writer(scal, keeps, sends, 0)
    g1, mixer_grad = backward_mixer(
        g[...], f_turned, gains, 0, scal, held, x1, gate, up, m, dgate, dup, h2_turned, put, store
    )
    done = backward_attention(
        g1, mixer_grad, x[...].T.astype(F32), gains, 0, scal, held, angles, wide, qkv, pt, ot,
        parts, h1_turned, o_turned, query_t, apad, vectors, put, store,
    )
    g_out[...] = done.T


def last_kernel(*refs):
    scal, sources, attend, query, key, value, output, mixer, gate, up, down, wide, rows = split(
        refs, 1, 8, 1, 1, 1, 1, 1, 1, 1, 1, 1, 1, 1
    )
    yl, core = scal[0], scal[1]
    for layer in range(2):

        @pl.when(pl.program_id(0) == layer)
        def _():
            tiles = [jnp.zeros((16, 128), F32)] * 2
            for core_rel in range(2):
                core_at = core ^ core_rel
                at = pl.ds(pl.multiple_of(core_at * 144, 16), 144)
                for slot in range(4):
                    source = sources[4 * layer + 2 * core_rel + slot // 2].at[slot % 2]
                    relative = slot if layer == 0 else (slot % 2) * 2 + slot // 2
                    j = relative ^ scal[2 + core_rel]
                    for t in range(3):
                        base = sum(TILES[:t])
                        lanes = pl.ds(pl.multiple_of((4 * t + j) * 128, 128), 128)
                        gate[0, at, lanes] = source[16 * base : 16 * base + 144, :].astype(F32)
                        up[0, at, lanes] = source[16 * base + 144 : 16 * base + 288, :].astype(F32)
                        wide[at, lanes] = source[16 * base + 432 : 16 * base + 576, :].astype(F32)
                        to = pl.ds(pl.multiple_of((2 * t + core_at) * 128, 128), 128)
                        down[0, pl.ds(pl.multiple_of(144 * j, 16), 144), to] = (
                            source[16 * base + 288 : 16 * base + 432, :].astype(F32)
                        )
                    tiles[core_rel] = jnp.where(j == 0, source[576:592, :].astype(F32), tiles[core_rel])
            query[0] = wide[:, 0:576]
            key[0] = wide[:, 576:768]
            value[0] = wide[:, 768:960]
            output[0] = wide[:, 960:1536]
            tile = jnp.where(core == 0, tiles[0], tiles[1])
            for c in range(5):
                size = min(128, WIDTH - 128 * c)
                rows[0:1, 128 * c : 128 * c + size] = tile[c : c + 1, 0:size]
                rows[1:2, 128 * c : 128 * c + size] = tile[c + 5 : c + 6, 0:size]
            share = jnp.where(yl == 0, rows[:, 0:288], rows[:, 288:576])
            attend[layer : layer + 1, :] = share[0:1, :]
            mixer[layer : layer + 1, :] = share[1:2, :]


SMEM = pl.BlockSpec(memory_space=pltpu.SMEM)
VMEM = pl.BlockSpec(memory_space=pltpu.VMEM)
HBM = pl.BlockSpec(memory_space=pl.ANY)
PARAMS = pltpu.CompilerParams(vmem_limit_bytes=VMEM_LIMIT)

FORWARD_STATE = (
    ((ROWS, 1024), BF16),
    ((3, ROWS, 3 * ROWS), BF16),
    ((WIDTH, ROWS), BF16),
    ((ROWS, WIDTH), F32),
    ((ROWS, FF), BF16),
    ((ROWS, FF), BF16),
    ((ROWS, FF), BF16),
)
MIXER_SCRATCH = [
    pltpu.VMEM((ROWS, FF), BF16),
    pltpu.VMEM((ROWS, FF), BF16),
    pltpu.VMEM((WIDTH, ROWS), BF16),
]
ATTENTION_SCRATCH = [
    pltpu.VMEM((ROWS, 1024), BF16),
    *[pltpu.VMEM((WIDTH, ROWS), BF16)] * 3,
    pltpu.VMEM((ROWS, 640), BF16),
    pltpu.VMEM((16, 128), F32),
]
WIDE = [pltpu.VMEM((ROWS, 1024), F32)]


def held_scratch(which=range(7)):
    return [pltpu.VMEM(WEIGHT_SHAPES[i], BF16) for i in which] + [pltpu.SemaphoreType.DMA((7,))]


def packed(*tiles):
    return [out((2, 2, 2, 16 * count, 128), BF16) for count in tiles * 2]


def out(shape, kind):
    return jax.ShapeDtypeStruct(shape, kind)


def cost(gflop, mbytes):
    return pl.CostEstimate(flops=int(gflop * 1e9), bytes_accessed=int(mbytes * 1e6), transcendentals=0)


def call_pack(layer, first, last, scal, own):
    return pl.pallas_call(
        functools.partial(pack_kernel, layer, first, last),
        out_shape=out((9 * (last - first), 16, 128), BF16),
        in_specs=[SMEM] + [HBM] * 7,
        out_specs=VMEM,
        scratch_shapes=[
            *[pltpu.VMEM((144, WEIGHT_SHAPES[i][1]), BF16) for i in range(6)],
            pltpu.VMEM((576, 384), BF16),
            pltpu.SemaphoreType.DMA((7,)),
        ],
        compiler_params=pltpu.CompilerParams(vmem_limit_bytes=PACK_VMEM),
        cost_estimate=cost(0, 4),
        name="pack",
    )(scal, *own)


def call_first(scal, x, gains, cosine, sine, bias, quarters, own):
    return pl.pallas_call(
        first_kernel,
        out_shape=[out((ROWS, WIDTH), F32)] + [out(*state) for state in FORWARD_STATE],
        in_specs=[SMEM] + [VMEM] * 9 + [HBM] * 7,
        out_specs=[VMEM] * 8,
        scratch_shapes=WIDE + held_scratch(),
        compiler_params=PARAMS,
        cost_estimate=cost(2.2, 16),
        name="first_forward",
    )(scal, x, gains, cosine, sine, bias, *quarters, *own)


def call_second(scal, x, cotangent, gains, angles, bias, quarters, own):
    return pl.pallas_call(
        second_kernel,
        out_shape=[out((WIDTH, ROWS), BF16), out((ROWS, WIDTH), F32)] + packed(*TILES),
        in_specs=[SMEM] + [VMEM] * 12 + [HBM] * 7,
        out_specs=[VMEM] * 8,
        scratch_shapes=[pltpu.VMEM(*state) for state in FORWARD_STATE]
        + MIXER_SCRATCH
        + ATTENTION_SCRATCH
        + WIDE
        + held_scratch(),
        compiler_params=PARAMS,
        cost_estimate=cost(7, 18),
        name="second_both",
    )(scal, x, cotangent, gains, *angles, bias, *quarters, *own)


def call_third(scal, x, g, gains, angles, quarters, states, own):
    return pl.pallas_call(
        third_kernel,
        out_shape=[out((WIDTH, ROWS), F32)] + packed(*TILES),
        in_specs=[SMEM] + [VMEM] * 18 + [HBM] * 7,
        out_specs=[VMEM] * 7,
        scratch_shapes=MIXER_SCRATCH
        + [pltpu.VMEM((WIDTH, ROWS), BF16)]
        + ATTENTION_SCRATCH
        + WIDE
        + held_scratch(),
        compiler_params=PARAMS,
        cost_estimate=cost(5, 22),
        name="first_backward",
    )(scal, x, g, gains, *angles, *quarters, *states, *own)


def call_last(scal, sources):
    gain = pl.BlockSpec((2, 288), lambda layer: (0, 0))
    shapes = [(288, 576), (288, 192), (288, 192), (288, 576), (288, 1536), (288, 1536), (576, 768)]
    matrices = [pl.BlockSpec((1, *s), lambda layer: (layer, 0, 0)) for s in shapes]
    outs = [out((2, *s), F32) for s in shapes]
    return pl.pallas_call(
        last_kernel,
        grid=(2,),
        out_shape=[out((2, 288), F32), *outs[:4], out((2, 288), F32), *outs[4:]],
        in_specs=[SMEM] + [pl.BlockSpec((2, 16 * sum(TILES), 128), lambda layer: (0, 0, 0))] * 8,
        out_specs=[gain, *matrices[:4], gain, *matrices[4:]],
        scratch_shapes=[pltpu.VMEM((288, FF), F32), pltpu.VMEM((2, WIDTH), F32)],
        compiler_params=LATE,
        cost_estimate=cost(0.1, 22),
        name="unpack",
    )(scal, *sources)


def tables(row):
    index = jnp.arange(ROWS, dtype=jnp.int32)
    fresh = jnp.concatenate([jnp.ones((1,), dtype=bool), row[1:] != row[:-1]])
    starts = lax.cummax(jnp.where(fresh, index, 0), axis=0)
    positions = (index - starts).astype(F32)
    frequency = ROPE_BASE ** (-(jnp.arange(HEAD // 2, dtype=F32) * 2.0 / HEAD))
    angles = positions[:, None] * frequency[None, :]
    cosine, sine = jnp.cos(angles), jnp.sin(angles)
    allowed = (row[:, None] == row[None, :]) & (index[:, None] <= index[None, :])
    bias = jnp.where(allowed, 0.0, MASKED).astype(F32)
    wide_sine = jnp.tile(jnp.concatenate([-sine, sine], axis=1), (1, 2))
    return (jnp.tile(cosine, (1, 4)), wide_sine, cosine.T, sine.T), bias


def ring_bits(at):
    high = at // 2
    return high ^ (at % 2), high


def halved(t, keeps, cames):
    def both(n):
        return jnp.concatenate([k[t][n] + c[t][n] for k, c in zip(keeps, cames)], axis=-2)

    total = both(0) + swap(both(1), STEPS[t][0])
    total = total[0] + swap(total[1], STEPS[t][1])
    return total[0] + swap(total[1], STEPS[t][2])


def summed(total, bits):
    code = 2 * bits["xv"] + bits["zv"]
    rows = total.shape[0] // 4

    def quarter(n):
        return lax.dynamic_slice_in_dim(total, (code ^ n) * rows, rows)

    came = [swap(quarter(n), move) for n, move in ((1, "zv"), (2, "xv"), (3, "xzv"))]
    mine = sum((a.astype(F32) for a in came), quarter(0).astype(F32)).astype(BF16)
    mine = mine + swap(mine, "yh")
    parts = [mine] + [swap(mine, move) for move in ("zv", "xv", "xzv")]
    low, high = bits["zv"] == 0, bits["xv"] == 0
    parts = [jnp.where(low, parts[n], parts[n ^ 1]) for n in range(4)]
    return jnp.concatenate([jnp.where(high, parts[n], parts[n ^ 2]) for n in range(4)])


def gathered(total, first, second):
    total = jnp.stack([total, swap(total, first)])
    far = swap(total, second)
    return total, far, swap(total, "core"), swap(far, "core")


def local(
    activations, seg_ids, cotangent, attend_gain, query_weight, key_matrix, value_matrix, output_weight,
    mixer_gain, gate_weight, up_weight, down_weight,
):
    z, yh, x, core, yl = (lax.axis_index(name) for name in ALL)
    (x_low, x_high), (z_low, z_high) = ring_bits(x), ring_bits(z)
    bits = {
        "xu": jnp.where(core == 0, x_low, x_high),
        "xv": jnp.where(core == 0, x_high, x_low),
        "zu": jnp.where(core == 0, z_low, z_high),
        "zv": jnp.where(core == 0, z_high, z_low),
    }
    scal = jnp.stack(
        [yl, core, 2 * bits["xu"] + bits["zu"], 2 * bits["xv"] + bits["zv"], x % 2]
    ).astype(jnp.int32)
    own = (
        query_weight, key_matrix, value_matrix, output_weight, gate_weight, up_weight,
        jnp.swapaxes(down_weight, 1, 2),
    )
    straight = [swap(call_pack(layer, *CHUNKS[layer][0], scal, own), "y") for layer in range(2)]
    gain_share = jnp.stack([attend_gain[0], mixer_gain[0], attend_gain[1], mixer_gain[1]])
    gain_other = swap(gain_share, "y")
    gains = jnp.where(
        yl == 0,
        jnp.concatenate([gain_share, gain_other], axis=1),
        jnp.concatenate([gain_other, gain_share], axis=1),
    ).astype(F32)
    angles, bias = tables(seg_ids[0])
    across = [swap(a, "xu") for a in straight]
    quarters_0 = (straight[0], across[0], swap(straight[0], "core"), swap(across[0], "core"))
    sibling_1 = swap(straight[1], "core")
    scal_first, sibling_1 = lax.optimization_barrier((scal, sibling_1))
    x_1, *states = call_first(scal_first, activations.T, gains, angles[0], angles[1], bias, quarters_0, own)
    x_1, across_1 = lax.optimization_barrier((x_1, across[1]))
    quarters_1 = (straight[1], across_1, sibling_1, swap(across_1, "core"))
    result, g, *packed_1 = call_second(scal, x_1, cotangent.T, gains, angles, bias, quarters_1, own)
    came_1 = [swap(a, "core") for a in packed_1[3:]]
    input_grad, *packed_0 = call_third(scal, activations.T, g, gains, angles, quarters_0, states, own)
    sends = lax.optimization_barrier((*packed_0[3:], *came_1))
    came_0, came_1 = [swap(a, "core") for a in sends[:3]], sends[3:]
    parts = [halved(t, (packed_0, packed_1), (came_0, came_1)) for t in range(3)]
    layers = [a[: 16 * TILES[t]] for t, a in enumerate(parts)] + [a[16 * TILES[t] :] for t, a in enumerate(parts)]
    total = summed(jnp.concatenate(layers), bits)
    half = total.shape[0] // 2
    sources = [*gathered(total[:half], "zu", "xu"), *gathered(total[half:], "xu", "zu")]
    grads = list(call_last(scal, sources))
    grads[8] = jnp.swapaxes(grads[8], 1, 2)
    return (result.T, input_grad.T, *grads)


def solution(mesh):
    fine = jax.sharding.Mesh(mesh.devices.reshape(SIZES), ALL)
    token, own = P(ALL, None), P(None, "yl")
    matrix = P(None, "yl", None)
    in_specs = (token, token, token, own, matrix, matrix, matrix, matrix, own, matrix, matrix, matrix)
    out_specs = (token, token, own, matrix, matrix, matrix, matrix, own, matrix, matrix, matrix)
    return jax.shard_map(local, mesh=fine, in_specs=in_specs, out_specs=out_specs, check_vma=False)
```
